32 devices in a mesh: dp: 8 (over z, y), mp: 4 (over x, core).
Axes of the slice: x: 2, y: 2, z: 4, core: 2. Of those that a mesh axis runs over, the one named last changes fastest.
Arguments:
- features: bfloat16 [24576, 1024], P('dp'), may hold values from -6 to 6
- curvature: bfloat16 [24576, 4096], P('dp', 'mp'), may hold values from 0.099609375 to 2
- task_grad: float32 [1024, 4096], P('dp', 'mp'), may hold values from -6 to 6
Outputs:
- solution: float32 [1024, 4096], P('dp', 'mp')
- residual: float32 [1024, 4096], P('dp', 'mp')
The draws below stay inside these ranges and needn't reach their ends.
All inputs are finite; a program needn't handle non-finite values.
Results may differ from the reference program's by a relative error of at most 0.0095.
The reference program's roundings to bfloat16 on the way count: a program that leaves them out, or rounds other values in their place, can miss the bound.
Values may be sent and summed in bfloat16 or wider, within the bound.
No kernel may reach another device: no remote copies, remote signals or barrier semaphores. Data moves between devices by JAX's collectives and lax.ppermute only.
A program may use at most 64 MiB of HBM per device.

```python
import math
import jax
import jax.numpy as jnp
from jax import lax

DIN = 1024
DOUT = 4096
TOK_DEV = 3072
ITERS = 2
TOKENS = 24576
N_DP = 8


def block_levels(key, extent, split, least, largest):
    factor_of = 1.0
    for axis_at, shards_of in split:
        heights = jax.random.uniform(jax.random.fold_in(jax.random.fold_in(key, 6), axis_at), (shards_of,), jnp.float32, least / len(split), largest / len(split))
        factor_of = factor_of * jnp.repeat(jnp.exp(heights), extent[axis_at] // shards_of).reshape((-1,) + (1,) * (len(extent) - 1 - axis_at))
    return factor_of


def bell_draw(rng, extent, deviation, most, pieces=(), dtype=jnp.bfloat16):
    loudness = block_levels(rng, extent, pieces, -0.22, 0.18) if pieces else 1.0
    result = jax.random.normal(rng, extent, jnp.float32) * deviation * loudness
    return jnp.minimum(jnp.maximum(result, -most), most).astype(dtype)


def setup_inputs(seed: int = 0) -> dict:
    key_list = jax.random.split(jax.random.key(seed), 4)
    return {
        "features": bell_draw(key_list[0], (TOKENS, DIN), 1.0, 6.0, ((0, 8),)),
        "curvature": jnp.clip(jnp.exp(math.log(2.0) - 2.9996462 * jax.random.uniform(key_list[1], (TOKENS, DOUT), jnp.float32) ** block_levels(key_list[1], (TOKENS, DOUT), ((0, 8), (1, 4)), -0.2, 0.2)), 0.099609375, 2.0).astype(jnp.bfloat16),
        "task_grad": bell_draw(key_list[2], (DIN, DOUT), 1.0, 6.0, ((0, 8), (1, 4)), jnp.float32),
    }


damp_coef = 0.5


def apply_operator(features, curvature, direction):
    dir_bf = direction.astype(jnp.bfloat16)
    feat_blocks = features.reshape(N_DP, TOK_DEV, DIN)
    curv_blocks = curvature.reshape(N_DP, TOK_DEV, DOUT)

    def add_block(accum, blocks):
        feat_rows, curv_rows = blocks
        projected = jnp.dot(feat_rows, dir_bf, preferred_element_type=jnp.float32)
        weighted = (curv_rows.astype(jnp.float32) * projected).astype(jnp.bfloat16)
        return accum + jnp.dot(feat_rows.T, weighted, preferred_element_type=jnp.float32), None

    accum, unused = lax.scan(add_block, jnp.zeros((DIN, DOUT), jnp.float32), (feat_blocks, curv_blocks))
    return accum / TOKENS + damp_coef * direction


def reference(features, curvature, task_grad):
    solution = jnp.zeros_like(task_grad)
    residual = task_grad
    direction = task_grad
    norm_now = jnp.sum(residual * residual)
    for turn in range(ITERS):
        curved = apply_operator(features, curvature, direction)
        step_len = norm_now / jnp.sum(direction * curved)
        solution = solution + step_len * direction
        residual = residual - step_len * curved
        if turn + 1 < ITERS:
            norm_next = jnp.sum(residual * residual)
            direction = residual + (norm_next / norm_now) * direction
            norm_now = norm_next
    return solution, residual
```

```python
import jax
import jax.numpy as jnp
from jax import lax
from jax.sharding import PartitionSpec as P

ITERS = 2
CHUNKS = 2

damp_coef = 0.5

FEATURE_MAX = 6.0
CURVATURE_MAX = 2.0
WIRE = jnp.float16
WIRE_MAX = 32768.0


def swap(values, axis, stride):
    size = lax.axis_size(axis)
    return lax.ppermute(values, axis, [(i, i ^ stride) for i in range(size)])


def strides_of(axis):
    size = lax.axis_size(axis)
    return [1 << bit for bit in reversed(range(size.bit_length() - 1))]


def global_sums(*values):
    total = jnp.stack(values)
    for axis in ("dp", "mp"):
        for stride in strides_of(axis):
            total = total + swap(total, axis, stride)
    return [total[i] for i in range(len(values))]


def gather_rows(block):
    for stride in strides_of("dp"):
        block = jnp.concatenate([block, swap(block, "dp", stride)], axis=0)
    return block


def block_order():
    order = [0]
    for stride in strides_of("dp"):
        order = order + [place ^ stride for place in order]
    return order


def scatter_rows(rows, scale):
    total = rows * scale
    for stride in reversed(strides_of("dp")):
        half = total.shape[0] // 2
        received = swap(total[half:].astype(WIRE), "dp", stride)
        total = total[:half] + received.astype(jnp.float32)
    return total / scale


def wire_scale(gathered, din):
    largest = jnp.max(jnp.abs(gathered.astype(jnp.float32)), axis=0, keepdims=True)
    bound = FEATURE_MAX * FEATURE_MAX * CURVATURE_MAX * din
    return WIRE_MAX / (bound * jnp.maximum(largest, 1e-30))


def shards(features, curvature, task_grad):
    n_dp = lax.axis_size("dp")
    token_count = features.shape[0] * n_dp
    din = features.shape[1]
    rows, cols = task_grad.shape
    width = cols // CHUNKS
    me = lax.axis_index("dp")
    spans = [slice(k * width, (k + 1) * width) for k in range(CHUNKS)]

    ordered = jnp.concatenate(
        [
            lax.dynamic_slice_in_dim(features, (me ^ place) * rows, rows, axis=1)
            for place in block_order()
        ],
        axis=1,
    )
    curv = [curvature[:, span] for span in spans]
    grad = [task_grad[:, span] for span in spans]

    def product(direction, k):
        gathered = gather_rows(direction.astype(jnp.bfloat16))
        projected = jnp.dot(ordered, gathered, preferred_element_type=jnp.float32)
        weighted = (curv[k] * projected).astype(jnp.bfloat16)
        partial = lax.dot_general(
            ordered, weighted, (((0,), (0,)), ((), ())), preferred_element_type=jnp.float32
        )
        partial = partial / token_count
        summed = scatter_rows(partial, wire_scale(gathered, din))
        return summed + damp_coef * direction, gathered, partial

    chunks = range(CHUNKS)
    norm_local = jnp.sum(task_grad * task_grad)
    image = [product(grad[k], k)[0] for k in chunks]
    curv_dot = sum(jnp.sum(grad[k] * image[k]) for k in chunks)
    image_dot = sum(jnp.sum(image[k] * image[k]) for k in chunks)
    norm_now, curv_dot, image_dot = global_sums(norm_local, curv_dot, image_dot)
    step_len = norm_now / curv_dot
    norm_next = norm_now - 2.0 * step_len * curv_dot + step_len * step_len * image_dot
    ratio = norm_next / norm_now
    residual = [grad[k] - step_len * image[k] for k in chunks]
    direction = [residual[k] + ratio * grad[k] for k in chunks]

    done = [product(direction[k], k) for k in chunks]
    dots = sum(
        jnp.sum(gathered.astype(jnp.float32) * partial) for _, gathered, partial in done
    ) + damp_coef * sum(jnp.sum(d * d) for d in direction)
    (curv_dot,) = global_sums(dots)
    last_len = norm_next / curv_dot
    solution = [step_len * grad[k] + last_len * direction[k] for k in chunks]
    residual = [residual[k] - last_len * done[k][0] for k in chunks]
    return jnp.concatenate(solution, axis=1), jnp.concatenate(residual, axis=1)


def solution(mesh):
    placed = (P("dp", None), P("dp", "mp"), P("dp", "mp"))
    return jax.shard_map(
        shards,
        mesh=mesh,
        in_specs=placed,
        out_specs=(P("dp", "mp"), P("dp", "mp")),
        check_vma=False,
    )
```

```python
import jax
import jax.numpy as jnp
from jax import lax
from jax.experimental import pallas as pl
from jax.experimental.pallas import tpu as pltpu
from jax.sharding import PartitionSpec as P

CHUNKS = 2
TILE = 768
VMEM_LIMIT = 56 * 2**20

damp_coef = 0.5

FEATURE_MAX = 6.0
CURVATURE_MAX = 2.0
WIRE = jnp.float16
WIRE_MAX = 32768.0
TINY = 1e-30
EXTRA = 16


def swap(values, axis, stride):
    size = lax.axis_size(axis)
    return lax.ppermute(values, axis, [(i, i ^ stride) for i in range(size)])


def strides_of(axis):
    size = lax.axis_size(axis)
    return [1 << bit for bit in reversed(range(size.bit_length() - 1))]


def routes():
    even = strides_of("dp")
    odd = even[:-2] + even[:-3:-1]
    return even, odd


def trade(values, step):
    n_dp, n_mp = lax.axis_size("dp"), lax.axis_size("mp")
    pairs = []
    for d in range(n_dp):
        for m in range(n_mp):
            pairs.append((d * n_mp + m, (d ^ routes()[m % 2][step]) * n_mp + m))
    return lax.ppermute(values, ("dp", "mp"), pairs)


def order_of(route):
    order = [0]
    for stride in route:
        order = order + [place ^ stride for place in order]
    return order


def join(halves):
    return jnp.concatenate(halves, axis=0)


def scatter_start(total, extra, step):
    half = total.shape[0] // 2
    sent = total[half:].astype(WIRE)
    if extra is not None:
        extra = extra.astype(WIRE)
        sent = join([sent, jnp.broadcast_to(extra, (EXTRA, extra.shape[1]))])
    return total[:half], extra, trade(sent, step)


def scatter_end(kept, extra, received):
    half = kept.shape[0]
    total = kept + received[:half].astype(jnp.float32)
    if extra is not None:
        extra = extra.astype(jnp.float32) + received[half : half + 1].astype(jnp.float32)
    return total, extra


def colsum(values):
    return jnp.sum(values, axis=0, keepdims=True)


def coef_kernel(sums_ref, *refs):
    out_ref = refs[-1]
    total = jnp.sum(sums_ref[...], axis=1, keepdims=True)
    norm, curv, image = total[0:1], total[1:2], total[2:3]
    step = norm / curv
    following = norm - 2.0 * step * curv + step * step * image
    ratio = following / norm
    width = sums_ref.shape[1]
    for k, (guess_ref, lift_ref) in enumerate(zip(refs[:-1:2], refs[1:-1:2])):
        along = step / guess_ref[...]
        out_ref[8 * k : 8 * k + 1, :] = along / lift_ref[...]
        out_ref[8 * k + 1 : 8 * k + 2, :] = 1.0 + ratio - along
        out_ref[8 * k + 2 : 8 * k + 3, :] = jnp.broadcast_to(step, (1, width))
        out_ref[8 * k + 3 : 8 * k + 4, :] = jnp.broadcast_to(1.0 + ratio, (1, width))
        out_ref[8 * k + 4 : 8 * k + 5, :] = jnp.broadcast_to(following, (1, width))


def curve_kernel(blocks, f_ref, c_ref, near_ref, far_ref, out_ref, stat_ref, held, total, *, n_dp, token_count):
    din = total.shape[0]
    rows = din // n_dp
    step = pl.program_id(0)
    last = pl.num_programs(0) - 1

    def place(position):
        return pl.ds(pl.multiple_of(blocks[position] * rows, rows), rows)

    @pl.when(step == 0)
    def _():
        for position in range(n_dp):
            half = (near_ref, far_ref)[2 * position // n_dp]
            at = (position % (n_dp // 2)) * rows
            held[place(position), :] = half[at : at + rows, :]

    projected = jnp.dot(f_ref[...], held[...], preferred_element_type=jnp.float32)
    weighted = (c_ref[...].astype(jnp.float32) * projected).astype(jnp.bfloat16)
    share = lax.dot_general(
        f_ref[...], weighted, (((0,), (0,)), ((), ())), preferred_element_type=jnp.float32
    )

    @pl.when(step == 0)
    def _():
        total[...] = share

    @pl.when(step > 0)
    def _():
        total[...] += share

    @pl.when(step == last)
    def _():
        vector = held[...].astype(jnp.float32)
        dot = jnp.sum(vector * total[...], axis=0, keepdims=True)
        largest = jnp.max(jnp.abs(vector), axis=0, keepdims=True)
        to_wire = WIRE_MAX / (bound_of(din) * token_count)
        square = jnp.sum(vector * vector, axis=0, keepdims=True)
        scale = to_wire / jnp.maximum(largest, TINY)
        stat_ref[0:1, :] = dot
        stat_ref[1:2, :] = largest
        stat_ref[2:3, :] = scale
        stat_ref[3:4, :] = dot / jnp.maximum(square, TINY) * to_wire
        for position in range(n_dp):
            out_ref[position * rows : (position + 1) * rows, :] = total[place(position), :] * scale


def bound_of(din):
    return FEATURE_MAX * FEATURE_MAX * CURVATURE_MAX * din


def curve(features, curvature, chunk, blocks, halves, n_dp):
    tokens, din = features.shape
    width = halves[0].shape[1]
    tile = TILE if tokens % TILE == 0 else tokens
    flops = 4 * tokens * din * width
    size = 2 * tokens * (din + width) + 6 * din * width
    half = pl.BlockSpec((din // 2, width), lambda i, blocks: (0, 0))
    return pl.pallas_call(
        lambda *refs: curve_kernel(*refs, n_dp=n_dp, token_count=n_dp * tokens),
        grid_spec=pltpu.PrefetchScalarGridSpec(
            num_scalar_prefetch=1,
            grid=(tokens // tile,),
            in_specs=[
                pl.BlockSpec((tile, din), lambda i, blocks: (i, 0)),
                pl.BlockSpec((tile, width), lambda i, blocks: (i, chunk)),
                half,
                half,
            ],
            out_specs=[
                pl.BlockSpec((din, width), lambda i, blocks: (0, 0)),
                pl.BlockSpec((8, width), lambda i, blocks: (0, 0)),
            ],
            scratch_shapes=[
                pltpu.VMEM((din, width), jnp.bfloat16),
                pltpu.VMEM((din, width), jnp.float32),
            ],
        ),
        out_shape=[
            jax.ShapeDtypeStruct((din, width), jnp.float32),
            jax.ShapeDtypeStruct((8, width), jnp.float32),
        ],
        compiler_params=pltpu.CompilerParams(vmem_limit_bytes=VMEM_LIMIT),
        cost_estimate=pl.CostEstimate(flops=flops, bytes_accessed=size, transcendentals=0),
    )(blocks, features, curvature, *halves)


def shards(features, curvature, task_grad):
    n_dp = lax.axis_size("dp")
    din = features.shape[1]
    token_count = features.shape[0] * n_dp
    width = task_grad.shape[1] // CHUNKS
    me = lax.axis_index("dp")
    odd = lax.axis_index("mp") % 2
    blocks = jnp.where(odd, *[jnp.array(order_of(r), jnp.int32) for r in routes()[::-1]]) ^ me
    steps = len(strides_of("dp"))
    chunks = range(CHUNKS)
    hops = []
    dots = None

    def multiply(k, halves):
        rows, stats = curve(features, curvature, k, blocks, halves, n_dp)
        return rows, stats

    def hop():
        nonlocal dots
        if hops:
            dots = dots + swap(dots, *hops.pop(0))

    grad = [task_grad[:, k * width : (k + 1) * width] for k in chunks]

    held = [g.astype(jnp.bfloat16) for g in grad]
    for step in range(steps):
        grad_rows = [(h, trade(h, step)) for h in held]
        if step + 1 < steps:
            held = [join(pair) for pair in grad_rows]

    stats, moving = [None] * CHUNKS, [None] * CHUNKS
    for k in chunks:
        rows, stats[k] = multiply(k, grad_rows[k])
        moving[k] = scatter_start(rows, stats[k][3:4], steps - 1)
    image, guess, lift = [None] * CHUNKS, [None] * CHUNKS, [None] * CHUNKS
    bound = bound_of(din)
    for step in reversed(range(steps)):
        for k in chunks:
            total, extra = scatter_end(*moving[k])
            if step:
                moving[k] = scatter_start(total, extra, step - 1)
                continue
            image[k] = total / (stats[k][2:3] * token_count) + damp_coef * grad[k]
            guess[k] = 1.0 / (extra * (bound / WIRE_MAX) + damp_coef)
            reach = jnp.maximum(stats[k][1:2], TINY) * (1.0 + 2.0 * (bound + 1.0))
            lift[k] = WIRE_MAX / reach
            trial = ((grad[k] - guess[k] * image[k]) * lift[k]).astype(WIRE)
            moving[k] = (trial, trade(trial, 0))

    dots = jnp.concatenate(
        [
            sum(colsum(grad[k] * grad[k]) for k in chunks),
            sum(colsum(grad[k] * image[k]) for k in chunks),
            sum(colsum(image[k] * image[k]) for k in chunks),
        ]
    )
    all_hops = [(axis, stride) for axis in ("dp", "mp") for stride in strides_of(axis)]
    hops = list(all_hops)
    per_step = -(-len(hops) // steps)
    tie = lax.optimization_barrier
    for step in range(1, steps):
        held = [join(pair) for pair in moving]
        moving = [(h, trade(h, step)) for h in held]
        for _ in range(per_step):
            hop()
    while hops:
        hop()
    coef = pl.pallas_call(
        coef_kernel, out_shape=jax.ShapeDtypeStruct((8 * CHUNKS, width), jnp.float32)
    )(dots, *[row for k in chunks for row in (guess[k], lift[k])])

    direction = []
    for k in chunks:
        row = coef[8 * k : 8 * k + 8]
        direction.append(row[3:4] * grad[k] - row[2:3] * image[k])
        halves = [
            (row[0:1] * t.astype(jnp.float32) + row[1:2] * g.astype(jnp.float32)).astype(
                jnp.bfloat16
            )
            for t, g in zip(moving[k], grad_rows[k])
        ]
        rows, stats[k] = multiply(k, halves)
        moving[k] = scatter_start(rows, None, steps - 1)

    dots = sum(s[0:1] for s in stats) / token_count
    dots += damp_coef * sum(colsum(d * d) for d in direction)
    hops = list(all_hops)
    hop()
    for step in reversed(range(steps)):
        for k in chunks:
            kept, _, received = moving[k]
            if hops:
                received, dots = tie((received, dots))
                hop()
            total, _ = scatter_end(kept, None, received)
            if step:
                moving[k] = scatter_start(total, None, step - 1)
            else:
                moving[k] = total / (stats[k][2:3] * token_count)
    while hops:
        hop()
    direction_dot = jnp.sum(dots, axis=1, keepdims=True)
    solution, residual = [], []
    for k in chunks:
        row = coef[8 * k : 8 * k + 8]
        last_len = row[4:5] / direction_dot
        curved = moving[k] + damp_coef * direction[k]
        solution.append(row[2:3] * grad[k] + last_len * direction[k])
        residual.append(grad[k] - row[2:3] * image[k] - last_len * curved)
    return jnp.concatenate(solution, axis=1), jnp.concatenate(residual, axis=1)


def solution(mesh):
    placed = (P("dp", None), P("dp", "mp"), P("dp", "mp"))
    return jax.shard_map(
        shards,
        mesh=mesh,
        in_specs=placed,
        out_specs=(P("dp", "mp"), P("dp", "mp")),
        check_vma=False,
    )
```

```python
import jax
import jax.numpy as jnp
from jax import lax
from jax.experimental import pallas as pl
from jax.experimental.pallas import tpu as pltpu
from jax.sharding import PartitionSpec as P

CHUNKS = 2
TILE = 1536
VMEM_LIMIT = 28 * 2**20

damp_coef = 0.5

FEATURE_MAX = 6.0
CURVATURE_MAX = 2.0
WIRE = jnp.float16
WIRE_MAX = 32768.0
TINY = 1e-30
EXTRA = 16


def swap(values, axis, stride):
    size = lax.axis_size(axis)
    return lax.ppermute(values, axis, [(i, i ^ stride) for i in range(size)])


def strides_of(axis):
    size = lax.axis_size(axis)
    return [1 << bit for bit in reversed(range(size.bit_length() - 1))]


def routes():
    even = strides_of("dp")
    odd = even[:-2] + even[:-3:-1]
    return even, odd


def trade(values, step):
    n_dp, n_mp = lax.axis_size("dp"), lax.axis_size("mp")
    pairs = []
    for d in range(n_dp):
        for m in range(n_mp):
            pairs.append((d * n_mp + m, (d ^ routes()[m % 2][step]) * n_mp + m))
    return lax.ppermute(values, ("dp", "mp"), pairs)


def order_of(route):
    order = [0]
    for stride in route:
        order = order + [place ^ stride for place in order]
    return order


def join(halves):
    return jnp.concatenate(halves, axis=0)


def scatter_start(total, extra, step):
    half = total.shape[0] // 2
    sent = total[half:].astype(WIRE)
    if extra is not None:
        extra = extra.astype(WIRE)
        sent = join([sent, jnp.broadcast_to(extra, (EXTRA, extra.shape[1]))])
    return total[:half], extra, trade(sent, step)


def scatter_end(kept, extra, received):
    half = kept.shape[0]
    total = kept + received[:half].astype(jnp.float32)
    if extra is not None:
        extra = extra.astype(jnp.float32) + received[half : half + 1].astype(jnp.float32)
    return total, extra


def colsum(values):
    return jnp.sum(values, axis=0, keepdims=True)


def coef_kernel(sums_ref, *refs):
    out_ref = refs[-1]
    total = jnp.sum(sums_ref[...], axis=1, keepdims=True)
    norm, curv, image = total[0:1], total[1:2], total[2:3]
    step = norm / curv
    following = norm - 2.0 * step * curv + step * step * image
    ratio = following / norm
    width = sums_ref.shape[1]
    for k, (guess_ref, lift_ref) in enumerate(zip(refs[:-1:2], refs[1:-1:2])):
        along = step / guess_ref[...]
        out_ref[8 * k : 8 * k + 1, :] = along / lift_ref[...]
        out_ref[8 * k + 1 : 8 * k + 2, :] = 1.0 + ratio - along
        out_ref[8 * k + 2 : 8 * k + 3, :] = jnp.broadcast_to(step, (1, width))
        out_ref[8 * k + 3 : 8 * k + 4, :] = jnp.broadcast_to(1.0 + ratio, (1, width))
        out_ref[8 * k + 4 : 8 * k + 5, :] = jnp.broadcast_to(following, (1, width))


def curve_kernel(blocks, f_ref, c_ref, near_ref, far_ref, out_ref, stat_ref, held, total, *, n_dp, token_count):
    din = total.shape[0]
    rows = din // n_dp
    step = pl.program_id(0)
    last = pl.num_programs(0) - 1

    def place(position):
        return pl.ds(pl.multiple_of(blocks[position] * rows, rows), rows)

    @pl.when(step == 0)
    def _():
        for position in range(n_dp):
            half = (near_ref, far_ref)[2 * position // n_dp]
            at = (position % (n_dp // 2)) * rows
            held[place(position), :] = half[at : at + rows, :]

    projected = jnp.dot(f_ref[...], held[...], preferred_element_type=jnp.float32)
    weighted = (c_ref[...].astype(jnp.float32) * projected).astype(jnp.bfloat16)
    share = lax.dot_general(
        f_ref[...], weighted, (((0,), (0,)), ((), ())), preferred_element_type=jnp.float32
    )

    @pl.when(step == 0)
    def _():
        total[...] = share

    @pl.when(step > 0)
    def _():
        total[...] += share

    @pl.when(step == last)
    def _():
        vector = held[...].astype(jnp.float32)
        dot = jnp.sum(vector * total[...], axis=0, keepdims=True)
        largest = jnp.max(jnp.abs(vector), axis=0, keepdims=True)
        to_wire = WIRE_MAX / (bound_of(din) * token_count)
        square = jnp.sum(vector * vector, axis=0, keepdims=True)
        scale = to_wire / jnp.maximum(largest, TINY)
        stat_ref[0:1, :] = dot
        stat_ref[1:2, :] = largest
        stat_ref[2:3, :] = scale
        stat_ref[3:4, :] = dot / jnp.maximum(square, TINY) * to_wire
        for position in range(n_dp):
            out_ref[position * rows : (position + 1) * rows, :] = total[place(position), :] * scale


def bound_of(din):
    return FEATURE_MAX * FEATURE_MAX * CURVATURE_MAX * din


def load_kernel(f_ref, c_ref, f_out, c_out, sems):
    copies = [
        pltpu.make_async_copy(f_ref, f_out, sems.at[0]),
        pltpu.make_async_copy(c_ref, c_out, sems.at[1]),
    ]
    for copy in copies:
        copy.start()
    for copy in copies:
        copy.wait()


def load(features, curvature):
    anywhere = pl.BlockSpec(memory_space=pl.ANY)
    size = 4 * (features.size + curvature.size)
    return pl.pallas_call(
        load_kernel,
        in_specs=[anywhere, anywhere],
        out_specs=[anywhere, anywhere],
        out_shape=[
            jax.ShapeDtypeStruct(features.shape, features.dtype),
            jax.ShapeDtypeStruct(curvature.shape, curvature.dtype),
        ],
        scratch_shapes=[pltpu.SemaphoreType.DMA((2,))],
        compiler_params=pltpu.CompilerParams(vmem_limit_bytes=2**20),
        cost_estimate=pl.CostEstimate(flops=0, bytes_accessed=size, transcendentals=0),
    )(features, curvature)


def curve(features, curvature, chunk, blocks, halves, n_dp):
    tokens, din = features.shape
    width = halves[0].shape[1]
    tile = TILE if tokens % TILE == 0 else tokens
    flops = 4 * tokens * din * width
    size = 2 * tokens * (din + width) + 6 * din * width
    half = pl.BlockSpec((din // 2, width), lambda i, blocks: (0, 0))
    return pl.pallas_call(
        lambda *refs: curve_kernel(*refs, n_dp=n_dp, token_count=n_dp * tokens),
        grid_spec=pltpu.PrefetchScalarGridSpec(
            num_scalar_prefetch=1,
            grid=(tokens // tile,),
            in_specs=[
                pl.BlockSpec((tile, din), lambda i, blocks: (i, 0)),
                pl.BlockSpec((tile, width), lambda i, blocks: (i, chunk)),
                half,
                half,
            ],
            out_specs=[
                pl.BlockSpec((din, width), lambda i, blocks: (0, 0)),
                pl.BlockSpec((8, width), lambda i, blocks: (0, 0)),
            ],
            scratch_shapes=[
                pltpu.VMEM((din, width), jnp.bfloat16),
                pltpu.VMEM((din, width), jnp.float32),
            ],
        ),
        out_shape=[
            jax.ShapeDtypeStruct((din, width), jnp.float32),
            jax.ShapeDtypeStruct((8, width), jnp.float32),
        ],
        compiler_params=pltpu.CompilerParams(vmem_limit_bytes=VMEM_LIMIT),
        cost_estimate=pl.CostEstimate(flops=flops, bytes_accessed=size, transcendentals=0),
    )(blocks, features, curvature, *halves)


def shards(features, curvature, task_grad):
    n_dp = lax.axis_size("dp")
    din = features.shape[1]
    token_count = features.shape[0] * n_dp
    width = task_grad.shape[1] // CHUNKS
    me = lax.axis_index("dp")
    odd = lax.axis_index("mp") % 2
    blocks = jnp.where(odd, *[jnp.array(order_of(r), jnp.int32) for r in routes()[::-1]]) ^ me
    steps = len(strides_of("dp"))
    chunks = range(CHUNKS)
    hops = []
    dots = None

    def multiply(k, halves):
        rows, stats = curve(features, curvature, k, blocks, halves, n_dp)
        return rows, stats

    tie = lax.optimization_barrier

    def in_step(moving):
        arrived = tie([m[-1] for m in moving])
        return [(*m[:-1], a) for m, a in zip(moving, arrived)]

    def hop():
        nonlocal dots
        if hops:
            dots = dots + swap(dots, *hops.pop(0))

    features, curvature = load(features, curvature)
    grad = [task_grad[:, k * width : (k + 1) * width] for k in chunks]

    held = [g.astype(jnp.bfloat16) for g in grad]
    for step in range(steps):
        grad_rows = [(h, trade(h, step)) for h in held]
        if step + 1 < steps:
            held = [join(pair) for pair in grad_rows]

    stats, moving = [None] * CHUNKS, [None] * CHUNKS
    for k in chunks:
        rows, stats[k] = multiply(k, grad_rows[k])
        moving[k] = scatter_start(rows, stats[k][3:4], steps - 1)
    image, guess, lift = [None] * CHUNKS, [None] * CHUNKS, [None] * CHUNKS
    bound = bound_of(din)
    for step in reversed(range(steps)):
        for k in chunks:
            total, extra = scatter_end(*moving[k])
            if step:
                moving[k] = scatter_start(total, extra, step - 1)
                moving[k : k + 2] = in_step(moving[k : k + 2])
                continue
            image[k] = total / (stats[k][2:3] * token_count) + damp_coef * grad[k]
            guess[k] = 1.0 / (extra * (bound / WIRE_MAX) + damp_coef)
            reach = jnp.maximum(stats[k][1:2], TINY) * (1.0 + 2.0 * (bound + 1.0))
            lift[k] = WIRE_MAX / reach
            trial = ((grad[k] - guess[k] * image[k]) * lift[k]).astype(WIRE)
            moving[k] = (trial, trade(trial, 0))
            moving[k : k + 2] = in_step(moving[k : k + 2])

    dots = jnp.concatenate(
        [
            sum(colsum(grad[k] * grad[k]) for k in chunks),
            sum(colsum(grad[k] * image[k]) for k in chunks),
            sum(colsum(image[k] * image[k]) for k in chunks),
        ]
    )
    all_hops = [(axis, stride) for axis in ("dp", "mp") for stride in strides_of(axis)]
    hops = list(all_hops)
    for step in range(1, steps):
        for k in chunks:
            held = join(moving[k])
            moving[k] = (held, trade(held, step))
            moving[k : k + 2] = in_step(moving[k : k + 2])
    while hops:
        hop()
    coef = pl.pallas_call(
        coef_kernel, out_shape=jax.ShapeDtypeStruct((8 * CHUNKS, width), jnp.float32)
    )(dots, *[row for k in chunks for row in (guess[k], lift[k])])

    direction = []
    for k in chunks:
        row = coef[8 * k : 8 * k + 8]
        direction.append(row[3:4] * grad[k] - row[2:3] * image[k])
        halves = [
            (row[0:1] * t.astype(jnp.float32) + row[1:2] * g.astype(jnp.float32)).astype(
                jnp.bfloat16
            )
            for t, g in zip(moving[k], grad_rows[k])
        ]
        rows, stats[k] = multiply(k, halves)
        moving[k] = scatter_start(rows, None, steps - 1)

    dots = sum(s[0:1] for s in stats) / token_count
    dots += damp_coef * sum(colsum(d * d) for d in direction)
    hops = list(all_hops)
    hop()
    for step in reversed(range(steps)):
        for k in chunks:
            kept, _, received = moving[k]
            if hops:
                received, dots = tie((received, dots))
                hop()
            total, _ = scatter_end(kept, None, received)
            if step:
                moving[k] = scatter_start(total, None, step - 1)
            else:
                moving[k] = total / (stats[k][2:3] * token_count)
    while hops:
        hop()
    direction_dot = jnp.sum(dots, axis=1, keepdims=True)
    solution, residual = [], []
    for k in chunks:
        row = coef[8 * k : 8 * k + 8]
        last_len = row[4:5] / direction_dot
        curved = moving[k] + damp_coef * direction[k]
        solution.append(row[2:3] * grad[k] + last_len * direction[k])
        residual.append(grad[k] - row[2:3] * image[k] - last_len * curved)
    return jnp.concatenate(solution, axis=1), jnp.concatenate(residual, axis=1)


def solution(mesh):
    placed = (P("dp", None), P("dp", "mp"), P("dp", "mp"))
    return jax.shard_map(
        shards,
        mesh=mesh,
        in_specs=placed,
        out_specs=(P("dp", "mp"), P("dp", "mp")),
        check_vma=False,
    )
```

```python
import jax
import jax.numpy as jnp
from jax import lax
from jax.experimental import pallas as pl
from jax.experimental.pallas import tpu as pltpu
from jax.sharding import PartitionSpec as P

CHUNKS = 2
TILE = 1536
VMEM_LIMIT = 28 * 2**20

damp_coef = 0.5

FEATURE_MAX = 6.0
CURVATURE_MAX = 2.0
WIRE = jnp.float16
WIRE_MAX = 32768.0
TINY = 1e-30
EXTRA = 16


def swap(values, axis, stride):
    size = lax.axis_size(axis)
    return lax.ppermute(values, axis, [(i, i ^ stride) for i in range(size)])


def strides_of(axis):
    size = lax.axis_size(axis)
    return [1 << bit for bit in reversed(range(size.bit_length() - 1))]


def routes():
    even = strides_of("dp")
    odd = even[:-2] + even[:-3:-1]
    return even, odd


def trade(values, step):
    n_dp, n_mp = lax.axis_size("dp"), lax.axis_size("mp")
    pairs = []
    for d in range(n_dp):
        for m in range(n_mp):
            pairs.append((d * n_mp + m, (d ^ routes()[m % 2][step]) * n_mp + m))
    return lax.ppermute(values, ("dp", "mp"), pairs)


def order_of(route):
    order = [0]
    for stride in route:
        order = order + [place ^ stride for place in order]
    return order


def join(halves):
    return jnp.concatenate(halves, axis=0)


def scatter_start(total, extra, step):
    half = total.shape[0] // 2
    sent = total[half:].astype(WIRE)
    if extra is not None:
        extra = extra.astype(WIRE)
        sent = join([sent, jnp.broadcast_to(extra, (EXTRA, extra.shape[1]))])
    return total[:half], extra, trade(sent, step)


def scatter_end(kept, extra, received):
    half = kept.shape[0]
    total = kept + received[:half].astype(jnp.float32)
    if extra is not None:
        extra = extra.astype(jnp.float32) + received[half : half + 1].astype(jnp.float32)
    return total, extra


def colsum(values):
    return jnp.sum(values, axis=0, keepdims=True)


def coef_kernel(sums_ref, *refs):
    out_ref = refs[-1]
    total = jnp.sum(sums_ref[...], axis=1, keepdims=True)
    norm, curv, image = total[0:1], total[1:2], total[2:3]
    step = norm / curv
    following = norm - 2.0 * step * curv + step * step * image
    ratio = following / norm
    width = sums_ref.shape[1]
    for k, (guess_ref, lift_ref) in enumerate(zip(refs[:-1:2], refs[1:-1:2])):
        along = step / guess_ref[...]
        out_ref[8 * k : 8 * k + 1, :] = along / lift_ref[...]
        out_ref[8 * k + 1 : 8 * k + 2, :] = 1.0 + ratio - along
        out_ref[8 * k + 2 : 8 * k + 3, :] = jnp.broadcast_to(step, (1, width))
        out_ref[8 * k + 3 : 8 * k + 4, :] = jnp.broadcast_to(1.0 + ratio, (1, width))
        out_ref[8 * k + 4 : 8 * k + 5, :] = jnp.broadcast_to(following, (1, width))


def curve_kernel(blocks, f_ref, c_ref, near_ref, far_ref, out_ref, stat_ref, held, total, *, n_dp, token_count):
    din = total.shape[0]
    rows = din // n_dp
    step = pl.program_id(0)
    last = pl.num_programs(0) - 1

    def place(position):
        return pl.ds(pl.multiple_of(blocks[position] * rows, rows), rows)

    @pl.when(step == 0)
    def _():
        for position in range(n_dp):
            half = (near_ref, far_ref)[2 * position // n_dp]
            at = (position % (n_dp // 2)) * rows
            held[place(position), :] = half[at : at + rows, :]

    projected = jnp.dot(f_ref[...], held[...], preferred_element_type=jnp.float32)
    weighted = (c_ref[...].astype(jnp.float32) * projected).astype(jnp.bfloat16)
    share = lax.dot_general(
        f_ref[...], weighted, (((0,), (0,)), ((), ())), preferred_element_type=jnp.float32
    )

    @pl.when(step == 0)
    def _():
        total[...] = share

    @pl.when(step > 0)
    def _():
        total[...] += share

    @pl.when(step == last)
    def _():
        vector = held[...].astype(jnp.float32)
        dot = jnp.sum(vector * total[...], axis=0, keepdims=True)
        largest = jnp.max(jnp.abs(vector), axis=0, keepdims=True)
        to_wire = WIRE_MAX / (bound_of(din) * token_count)
        square = jnp.sum(vector * vector, axis=0, keepdims=True)
        scale = to_wire / jnp.maximum(largest, TINY)
        stat_ref[0:1, :] = dot
        stat_ref[1:2, :] = largest
        stat_ref[2:3, :] = scale
        stat_ref[3:4, :] = dot / jnp.maximum(square, TINY) * to_wire
        for position in range(n_dp):
            out_ref[position * rows : (position + 1) * rows, :] = total[place(position), :] * scale


def bound_of(din):
    return FEATURE_MAX * FEATURE_MAX * CURVATURE_MAX * din


def load_kernel(f_ref, c_ref, f_out, c_out, sems):
    copies = [
        pltpu.make_async_copy(f_ref, f_out, sems.at[0]),
        pltpu.make_async_copy(c_ref, c_out, sems.at[1]),
    ]
    for copy in copies:
        copy.start()
    for copy in copies:
        copy.wait()


def load(features, curvature):
    anywhere = pl.BlockSpec(memory_space=pl.ANY)
    size = 4 * (features.size + curvature.size)
    return pl.pallas_call(
        load_kernel,
        in_specs=[anywhere, anywhere],
        out_specs=[anywhere, anywhere],
        out_shape=[
            jax.ShapeDtypeStruct(features.shape, features.dtype),
            jax.ShapeDtypeStruct(curvature.shape, curvature.dtype),
        ],
        scratch_shapes=[pltpu.SemaphoreType.DMA((2,))],
        compiler_params=pltpu.CompilerParams(vmem_limit_bytes=2**20),
        cost_estimate=pl.CostEstimate(flops=0, bytes_accessed=size, transcendentals=0),
    )(features, curvature)


def curve(features, curvature, chunk, blocks, halves, n_dp):
    tokens, din = features.shape
    width = halves[0].shape[1]
    tile = TILE if tokens % TILE == 0 else tokens
    flops = 4 * tokens * din * width
    size = 2 * tokens * (din + width) + 6 * din * width
    half = pl.BlockSpec((din // 2, width), lambda i, blocks: (0, 0))
    return pl.pallas_call(
        lambda *refs: curve_kernel(*refs, n_dp=n_dp, token_count=n_dp * tokens),
        grid_spec=pltpu.PrefetchScalarGridSpec(
            num_scalar_prefetch=1,
            grid=(tokens // tile,),
            in_specs=[
                pl.BlockSpec((tile, din), lambda i, blocks: (i, 0)),
                pl.BlockSpec((tile, width), lambda i, blocks: (i, chunk)),
                half,
                half,
            ],
            out_specs=[
                pl.BlockSpec((din, width), lambda i, blocks: (0, 0)),
                pl.BlockSpec((8, width), lambda i, blocks: (0, 0)),
            ],
            scratch_shapes=[
                pltpu.VMEM((din, width), jnp.bfloat16),
                pltpu.VMEM((din, width), jnp.float32),
            ],
        ),
        out_shape=[
            jax.ShapeDtypeStruct((din, width), jnp.float32),
            jax.ShapeDtypeStruct((8, width), jnp.float32),
        ],
        compiler_params=pltpu.CompilerParams(vmem_limit_bytes=VMEM_LIMIT),
        cost_estimate=pl.CostEstimate(flops=flops, bytes_accessed=size, transcendentals=0),
    )(blocks, features, curvature, *halves)


def shards(features, curvature, task_grad):
    n_dp = lax.axis_size("dp")
    din = features.shape[1]
    token_count = features.shape[0] * n_dp
    width = task_grad.shape[1] // CHUNKS
    me = lax.axis_index("dp")
    odd = lax.axis_index("mp") % 2
    blocks = jnp.where(odd, *[jnp.array(order_of(r), jnp.int32) for r in routes()[::-1]]) ^ me
    steps = len(strides_of("dp"))
    chunks = range(CHUNKS)
    hops = []
    dots = None

    def multiply(k, halves):
        rows, stats = curve(features, curvature, k, blocks, halves, n_dp)
        return rows, stats

    tie = lax.optimization_barrier

    def in_step(moving):
        arrived = tie([m[-1] for m in moving])
        return [(*m[:-1], a) for m, a in zip(moving, arrived)]

    def hop():
        nonlocal dots
        if hops:
            dots = dots + swap(dots, *hops.pop(0))

    features, curvature = load(features, curvature)
    grad = [task_grad[:, k * width : (k + 1) * width] for k in chunks]

    held = [g.astype(jnp.bfloat16) for g in grad]
    for step in range(steps):
        grad_rows = [(h, trade(h, step)) for h in held]
        if step + 1 < steps:
            held = [join(pair) for pair in grad_rows]

    stats, moving = [None] * CHUNKS, [None] * CHUNKS
    for k in chunks:
        rows, stats[k] = multiply(k, grad_rows[k])
        moving[k] = scatter_start(rows, stats[k][3:4], steps - 1)
    image, guess, lift = [None] * CHUNKS, [None] * CHUNKS, [None] * CHUNKS
    bound = bound_of(din)
    for step in reversed(range(steps)):
        for k in chunks:
            total, extra = scatter_end(*moving[k])
            if step:
                moving[k] = scatter_start(total, extra, step - 1)
                moving[k : k + 2] = in_step(moving[k : k + 2])
                continue
            image[k] = total / (stats[k][2:3] * token_count) + damp_coef * grad[k]
            guess[k] = 1.0 / (extra * (bound / WIRE_MAX) + damp_coef)
            reach = jnp.maximum(stats[k][1:2], TINY) * (1.0 + 2.0 * (bound + 1.0))
            lift[k] = WIRE_MAX / reach
            trial = ((grad[k] - guess[k] * image[k]) * lift[k]).astype(WIRE)
            moving[k] = (trial, trade(trial, 0))
            moving[k : k + 2] = in_step(moving[k : k + 2])

    dots = jnp.concatenate(
        [
            sum(colsum(grad[k] * grad[k]) for k in chunks),
            sum(colsum(grad[k] * image[k]) for k in chunks),
            sum(colsum(image[k] * image[k]) for k in chunks),
        ]
    )
    all_hops = [(axis, stride) for axis in ("mp", "dp") for stride in reversed(strides_of(axis))]
    hops = list(all_hops)
    for step in range(1, steps):
        for k in chunks:
            held = join(moving[k])
            moving[k] = (held, trade(held, step))
            moving[k : k + 2] = in_step(moving[k : k + 2])
    for _ in range(3):
        hop()
    arrived, dots = tie((moving[0][-1], dots))
    moving[0] = (*moving[0][:-1], arrived)
    while hops:
        hop()
    coef = pl.pallas_call(
        coef_kernel, out_shape=jax.ShapeDtypeStruct((8 * CHUNKS, width), jnp.float32)
    )(dots, *[row for k in chunks for row in (guess[k], lift[k])])

    direction = []
    for k in chunks:
        row = coef[8 * k : 8 * k + 8]
        direction.append(row[3:4] * grad[k] - row[2:3] * image[k])
        halves = [
            (row[0:1] * t.astype(jnp.float32) + row[1:2] * g.astype(jnp.float32)).astype(
                jnp.bfloat16
            )
            for t, g in zip(moving[k], grad_rows[k])
        ]
        rows, stats[k] = multiply(k, halves)
        moving[k] = scatter_start(rows, None, steps - 1)

    dots = sum(s[0:1] for s in stats) / token_count
    dots += damp_coef * sum(colsum(d * d) for d in direction)
    hops = list(all_hops)
    hop()
    for step in reversed(range(steps)):
        for k in chunks:
            kept, _, received = moving[k]
            if hops:
                received, dots = tie((received, dots))
                hop()
            total, _ = scatter_end(kept, None, received)
            if step:
                moving[k] = scatter_start(total, None, step - 1)
            else:
                moving[k] = total / (stats[k][2:3] * token_count)
    while hops:
        hop()
    direction_dot = jnp.sum(dots, axis=1, keepdims=True)
    solution, residual = [], []
    for k in chunks:
        row = coef[8 * k : 8 * k + 8]
        last_len = row[4:5] / direction_dot
        curved = moving[k] + damp_coef * direction[k]
        solution.append(row[2:3] * grad[k] + last_len * direction[k])
        residual.append(grad[k] - row[2:3] * image[k] - last_len * curved)
    return jnp.concatenate(solution, axis=1), jnp.concatenate(residual, axis=1)


def solution(mesh):
    placed = (P("dp", None), P("dp", "mp"), P("dp", "mp"))
    return jax.shard_map(
        shards,
        mesh=mesh,
        in_specs=placed,
        out_specs=(P("dp", "mp"), P("dp", "mp")),
        check_vma=False,
    )
```

```python
import jax
import jax.numpy as jnp
from jax import lax
from jax.experimental import pallas as pl
from jax.experimental.pallas import tpu as pltpu
from jax.sharding import PartitionSpec as P

CHUNKS = 2
TILE = 1536
VMEM_LIMIT = 28 * 2**20

damp_coef = 0.5

FEATURE_MAX = 6.0
CURVATURE_MAX = 2.0
WIRE = jnp.float16
WIRE_MAX = 32768.0
TINY = 1e-30
EXTRA = 16


def swap(values, axis, stride):
    size = lax.axis_size(axis)
    return lax.ppermute(values, axis, [(i, i ^ stride) for i in range(size)])


def strides_of(axis):
    size = lax.axis_size(axis)
    return [1 << bit for bit in reversed(range(size.bit_length() - 1))]


def routes():
    even = strides_of("dp")
    odd = even[:-2] + even[:-3:-1]
    return even, odd


def trade(values, step):
    n_dp, n_mp = lax.axis_size("dp"), lax.axis_size("mp")
    pairs = []
    for d in range(n_dp):
        for m in range(n_mp):
            pairs.append((d * n_mp + m, (d ^ routes()[m % 2][step]) * n_mp + m))
    return lax.ppermute(values, ("dp", "mp"), pairs)


def order_of(route):
    order = [0]
    for stride in route:
        order = order + [place ^ stride for place in order]
    return order


def join(halves):
    return jnp.concatenate(halves, axis=0)


def scatter_start(total, extra, step):
    half = total.shape[0] // 2
    sent = total[half:].astype(WIRE)
    if extra is not None:
        extra = extra.astype(WIRE)
        sent = join([sent, jnp.broadcast_to(extra, (EXTRA, extra.shape[1]))])
    return total[:half], extra, trade(sent, step)


def scatter_end(kept, extra, received):
    half = kept.shape[0]
    total = kept + received[:half].astype(jnp.float32)
    if extra is not None:
        extra = extra.astype(jnp.float32) + received[half : half + 1].astype(jnp.float32)
    return total, extra


def colsum(values):
    return jnp.sum(values, axis=0, keepdims=True)


def coef_kernel(sums_ref, *refs):
    out_ref = refs[-1]
    total = jnp.sum(sums_ref[...], axis=1, keepdims=True)
    norm, curv, image = total[0:1], total[1:2], total[2:3]
    step = norm / curv
    following = norm - 2.0 * step * curv + step * step * image
    ratio = following / norm
    width = sums_ref.shape[1]
    for k, (guess_ref, lift_ref) in enumerate(zip(refs[:-1:2], refs[1:-1:2])):
        along = step / guess_ref[...]
        out_ref[8 * k : 8 * k + 1, :] = along / lift_ref[...]
        out_ref[8 * k + 1 : 8 * k + 2, :] = 1.0 + ratio - along
        out_ref[8 * k + 2 : 8 * k + 3, :] = jnp.broadcast_to(step, (1, width))
        out_ref[8 * k + 3 : 8 * k + 4, :] = jnp.broadcast_to(1.0 + ratio, (1, width))
        out_ref[8 * k + 4 : 8 * k + 5, :] = jnp.broadcast_to(following, (1, width))


def curve_kernel(blocks, f_ref, c_ref, near_ref, far_ref, out_ref, stat_ref, held, total, *, n_dp, token_count):
    din = total.shape[0]
    rows = din // n_dp
    step = pl.program_id(0)
    last = pl.num_programs(0) - 1

    def place(position):
        return pl.ds(pl.multiple_of(blocks[position] * rows, rows), rows)

    @pl.when(step == 0)
    def _():
        for position in range(n_dp):
            half = (near_ref, far_ref)[2 * position // n_dp]
            at = (position % (n_dp // 2)) * rows
            held[place(position), :] = half[at : at + rows, :]

    projected = jnp.dot(f_ref[...], held[...], preferred_element_type=jnp.float32)
    weighted = (c_ref[...].astype(jnp.float32) * projected).astype(jnp.bfloat16)
    share = lax.dot_general(
        f_ref[...], weighted, (((0,), (0,)), ((), ())), preferred_element_type=jnp.float32
    )

    @pl.when(step == 0)
    def _():
        total[...] = share

    @pl.when(step > 0)
    def _():
        total[...] += share

    @pl.when(step == last)
    def _():
        vector = held[...].astype(jnp.float32)
        dot = jnp.sum(vector * total[...], axis=0, keepdims=True)
        largest = jnp.max(jnp.abs(vector), axis=0, keepdims=True)
        to_wire = WIRE_MAX / (bound_of(din) * token_count)
        square = jnp.sum(vector * vector, axis=0, keepdims=True)
        scale = to_wire / jnp.maximum(largest, TINY)
        stat_ref[0:1, :] = dot
        stat_ref[1:2, :] = largest
        stat_ref[2:3, :] = scale
        stat_ref[3:4, :] = dot / jnp.maximum(square, TINY) * to_wire
        for position in range(n_dp):
            out_ref[position * rows : (position + 1) * rows, :] = total[place(position), :] * scale


def bound_of(din):
    return FEATURE_MAX * FEATURE_MAX * CURVATURE_MAX * din


def load_kernel(f_ref, c_ref, f_out, c_out, sems):
    copies = [
        pltpu.make_async_copy(f_ref, f_out, sems.at[0]),
        pltpu.make_async_copy(c_ref, c_out, sems.at[1]),
    ]
    for copy in copies:
        copy.start()
    for copy in copies:
        copy.wait()


def load(features, curvature):
    anywhere = pl.BlockSpec(memory_space=pl.ANY)
    size = 4 * (features.size + curvature.size)
    return pl.pallas_call(
        load_kernel,
        in_specs=[anywhere, anywhere],
        out_specs=[anywhere, anywhere],
        out_shape=[
            jax.ShapeDtypeStruct(features.shape, features.dtype),
            jax.ShapeDtypeStruct(curvature.shape, curvature.dtype),
        ],
        scratch_shapes=[pltpu.SemaphoreType.DMA((2,))],
        compiler_params=pltpu.CompilerParams(vmem_limit_bytes=2**20),
        cost_estimate=pl.CostEstimate(flops=0, bytes_accessed=size, transcendentals=0),
    )(features, curvature)


def curve(features, curvature, chunk, blocks, halves, n_dp):
    tokens, din = features.shape
    width = halves[0].shape[1]
    tile = TILE if tokens % TILE == 0 else tokens
    flops = 4 * tokens * din * width
    size = 2 * tokens * (din + width) + 6 * din * width
    half = pl.BlockSpec((din // 2, width), lambda i, blocks: (0, 0))
    return pl.pallas_call(
        lambda *refs: curve_kernel(*refs, n_dp=n_dp, token_count=n_dp * tokens),
        grid_spec=pltpu.PrefetchScalarGridSpec(
            num_scalar_prefetch=1,
            grid=(tokens // tile,),
            in_specs=[
                pl.BlockSpec((tile, din), lambda i, blocks: (i, 0)),
                pl.BlockSpec((tile, width), lambda i, blocks: (i, chunk)),
                half,
                half,
            ],
            out_specs=[
                pl.BlockSpec((din, width), lambda i, blocks: (0, 0)),
                pl.BlockSpec((8, width), lambda i, blocks: (0, 0)),
            ],
            scratch_shapes=[
                pltpu.VMEM((din, width), jnp.bfloat16),
                pltpu.VMEM((din, width), jnp.float32),
            ],
        ),
        out_shape=[
            jax.ShapeDtypeStruct((din, width), jnp.float32),
            jax.ShapeDtypeStruct((8, width), jnp.float32),
        ],
        compiler_params=pltpu.CompilerParams(vmem_limit_bytes=VMEM_LIMIT),
        cost_estimate=pl.CostEstimate(flops=flops, bytes_accessed=size, transcendentals=0),
    )(blocks, features, curvature, *halves)


def shards(features, curvature, task_grad):
    n_dp = lax.axis_size("dp")
    din = features.shape[1]
    token_count = features.shape[0] * n_dp
    width = task_grad.shape[1] // CHUNKS
    me = lax.axis_index("dp")
    odd = lax.axis_index("mp") % 2
    blocks = jnp.where(odd, *[jnp.array(order_of(r), jnp.int32) for r in routes()[::-1]]) ^ me
    steps = len(strides_of("dp"))
    chunks = range(CHUNKS)
    hops = []
    dots = None

    def multiply(k, halves):
        rows, stats = curve(features, curvature, k, blocks, halves, n_dp)
        return rows, stats

    tie = lax.optimization_barrier

    def in_step(moving):
        arrived = tie([m[-1] for m in moving])
        return [(*m[:-1], a) for m, a in zip(moving, arrived)]

    def hop():
        nonlocal dots
        if hops:
            dots = dots + swap(dots, *hops.pop(0))

    features, curvature = load(features, curvature)
    grad = [task_grad[:, k * width : (k + 1) * width] for k in chunks]

    held = [g.astype(jnp.bfloat16) for g in grad]
    for step in range(steps):
        grad_rows = [(h, trade(h, step)) for h in held]
        if step + 1 < steps:
            held = [join(pair) for pair in grad_rows]

    stats, moving = [None] * CHUNKS, [None] * CHUNKS
    for k in chunks:
        rows, stats[k] = multiply(k, grad_rows[k])
        moving[k] = scatter_start(rows, stats[k][3:4], steps - 1)
    image, guess, lift = [None] * CHUNKS, [None] * CHUNKS, [None] * CHUNKS
    bound = bound_of(din)
    for step in reversed(range(steps)):
        for k in chunks:
            total, extra = scatter_end(*moving[k])
            if step:
                moving[k] = scatter_start(total, extra, step - 1)
                moving[k : k + 2] = in_step(moving[k : k + 2])
                continue
            image[k] = total / (stats[k][2:3] * token_count) + damp_coef * grad[k]
            guess[k] = 1.0 / (extra * (bound / WIRE_MAX) + damp_coef)
            reach = jnp.maximum(stats[k][1:2], TINY) * (1.0 + 2.0 * (bound + 1.0))
            lift[k] = WIRE_MAX / reach
            trial = ((grad[k] - guess[k] * image[k]) * lift[k]).astype(WIRE)
            moving[k] = (trial, trade(trial, 0))
            moving[k : k + 2] = in_step(moving[k : k + 2])

    dots = jnp.concatenate(
        [
            sum(colsum(grad[k] * grad[k]) for k in chunks),
            sum(colsum(grad[k] * image[k]) for k in chunks),
            sum(colsum(image[k] * image[k]) for k in chunks),
        ]
    )
    all_hops = [(axis, stride) for axis in ("mp", "dp") for stride in reversed(strides_of(axis))]
    hops = list(all_hops)
    for step in range(1, steps):
        for k in chunks:
            held = join(moving[k])
            moving[k] = (held, trade(held, step))
            moving[k : k + 2] = in_step(moving[k : k + 2])
    while hops:
        hop()
    coef = pl.pallas_call(
        coef_kernel, out_shape=jax.ShapeDtypeStruct((8 * CHUNKS, width), jnp.float32)
    )(dots, *[row for k in chunks for row in (guess[k], lift[k])])

    direction = []
    for k in chunks:
        row = coef[8 * k : 8 * k + 8]
        direction.append(row[3:4] * grad[k] - row[2:3] * image[k])
        halves = [
            (row[0:1] * t.astype(jnp.float32) + row[1:2] * g.astype(jnp.float32)).astype(
                jnp.bfloat16
            )
            for t, g in zip(moving[k], grad_rows[k])
        ]
        rows, stats[k] = multiply(k, halves)
        moving[k] = scatter_start(rows, None, steps - 1)

    dots = sum(s[0:1] for s in stats) / token_count
    dots += damp_coef * sum(colsum(d * d) for d in direction)
    hops = list(all_hops)
    hop()
    for step in reversed(range(steps)):
        for k in chunks:
            kept, _, received = moving[k]
            if hops:
                received, dots = tie((received, dots))
                hop()
            total, _ = scatter_end(kept, None, received)
            if step:
                moving[k] = scatter_start(total, None, step - 1)
            else:
                moving[k] = total / (stats[k][2:3] * token_count)
    while hops:
        hop()
    direction_dot = jnp.sum(dots, axis=1, keepdims=True)
    solution, residual = [], []
    for k in chunks:
        row = coef[8 * k : 8 * k + 8]
        last_len = row[4:5] / direction_dot
        curved = moving[k] + damp_coef * direction[k]
        solution.append(row[2:3] * grad[k] + last_len * direction[k])
        residual.append(grad[k] - row[2:3] * image[k] - last_len * curved)
    return jnp.concatenate(solution, axis=1), jnp.concatenate(residual, axis=1)


def solution(mesh):
    placed = (P("dp", None), P("dp", "mp"), P("dp", "mp"))
    return jax.shard_map(
        shards,
        mesh=mesh,
        in_specs=placed,
        out_specs=(P("dp", "mp"), P("dp", "mp")),
        check_vma=False,
    )
```

```python
import jax
import jax.numpy as jnp
from jax import lax
from jax.experimental import pallas as pl
from jax.experimental.pallas import tpu as pltpu
from jax.sharding import PartitionSpec as P

CHUNKS = 2
TILE = 1536
VMEM_LIMIT = 28 * 2**20

damp_coef = 0.5

FEATURE_MAX = 6.0
CURVATURE_MAX = 2.0
WIRE = jnp.float16
WIRE_MAX = 32768.0
TINY = 1e-30
EXTRA = 16


def swap(values, axis, stride):
    size = lax.axis_size(axis)
    return lax.ppermute(values, axis, [(i, i ^ stride) for i in range(size)])


def strides_of(axis):
    size = lax.axis_size(axis)
    return [1 << bit for bit in reversed(range(size.bit_length() - 1))]


def routes():
    even = strides_of("dp")
    odd = even[:-2] + even[:-3:-1]
    return even, odd


def trade(values, step):
    n_dp, n_mp = lax.axis_size("dp"), lax.axis_size("mp")
    pairs = []
    for d in range(n_dp):
        for m in range(n_mp):
            pairs.append((d * n_mp + m, (d ^ routes()[m % 2][step]) * n_mp + m))
    return lax.ppermute(values, ("dp", "mp"), pairs)


def order_of(route):
    order = [0]
    for stride in route:
        order = order + [place ^ stride for place in order]
    return order


def join(halves):
    return jnp.concatenate(halves, axis=0)


def scatter_start(total, extra, step):
    half = total.shape[0] // 2
    sent = total[half:].astype(WIRE)
    if extra is not None:
        extra = extra.astype(WIRE)
        sent = join([sent, jnp.broadcast_to(extra, (EXTRA, extra.shape[1]))])
    return total[:half], extra, trade(sent, step)


def scatter_end(kept, extra, received):
    half = kept.shape[0]
    total = kept + received[:half].astype(jnp.float32)
    if extra is not None:
        extra = extra.astype(jnp.float32) + received[half : half + 1].astype(jnp.float32)
    return total, extra


def colsum(values):
    return jnp.sum(values, axis=0, keepdims=True)


def coef_kernel(sums_ref, *refs):
    out_ref = refs[-1]
    total = jnp.sum(sums_ref[...], axis=1, keepdims=True)
    norm, curv, image = total[0:1], total[1:2], total[2:3]
    step = norm / curv
    following = norm - 2.0 * step * curv + step * step * image
    ratio = following / norm
    width = sums_ref.shape[1]
    for k, (guess_ref, lift_ref) in enumerate(zip(refs[:-1:2], refs[1:-1:2])):
        along = step / guess_ref[...]
        out_ref[8 * k : 8 * k + 1, :] = along / lift_ref[...]
        out_ref[8 * k + 1 : 8 * k + 2, :] = 1.0 + ratio - along
        out_ref[8 * k + 2 : 8 * k + 3, :] = jnp.broadcast_to(step, (1, width))
        out_ref[8 * k + 3 : 8 * k + 4, :] = jnp.broadcast_to(1.0 + ratio, (1, width))
        out_ref[8 * k + 4 : 8 * k + 5, :] = jnp.broadcast_to(following, (1, width))


def curve_kernel(blocks, f_ref, c_ref, near_ref, far_ref, out_ref, stat_ref, held, total, *, n_dp, token_count):
    din = total.shape[0]
    rows = din // n_dp
    step = pl.program_id(0)
    last = pl.num_programs(0) - 1

    def place(position):
        return pl.ds(pl.multiple_of(blocks[position] * rows, rows), rows)

    @pl.when(step == 0)
    def _():
        for position in range(n_dp):
            half = (near_ref, far_ref)[2 * position // n_dp]
            at = (position % (n_dp // 2)) * rows
            held[place(position), :] = half[at : at + rows, :]

    projected = jnp.dot(f_ref[...], held[...], preferred_element_type=jnp.float32)
    weighted = (c_ref[...].astype(jnp.float32) * projected).astype(jnp.bfloat16)
    share = lax.dot_general(
        f_ref[...], weighted, (((0,), (0,)), ((), ())), preferred_element_type=jnp.float32
    )

    @pl.when(step == 0)
    def _():
        total[...] = share

    @pl.when(step > 0)
    def _():
        total[...] += share

    @pl.when(step == last)
    def _():
        vector = held[...].astype(jnp.float32)
        dot = jnp.sum(vector * total[...], axis=0, keepdims=True)
        largest = jnp.max(jnp.abs(vector), axis=0, keepdims=True)
        to_wire = WIRE_MAX / (bound_of(din) * token_count)
        square = jnp.sum(vector * vector, axis=0, keepdims=True)
        scale = to_wire / jnp.maximum(largest, TINY)
        stat_ref[0:1, :] = dot
        stat_ref[1:2, :] = largest
        stat_ref[2:3, :] = scale
        stat_ref[3:4, :] = dot / jnp.maximum(square, TINY) * to_wire
        for position in range(n_dp):
            out_ref[position * rows : (position + 1) * rows, :] = total[place(position), :] * scale


def bound_of(din):
    return FEATURE_MAX * FEATURE_MAX * CURVATURE_MAX * din


def load_kernel(f_ref, c_ref, f_out, c_out, sems):
    copies = [
        pltpu.make_async_copy(f_ref, f_out, sems.at[0]),
        pltpu.make_async_copy(c_ref, c_out, sems.at[1]),
    ]
    for copy in copies:
        copy.start()
    for copy in copies:
        copy.wait()


def load(features, curvature):
    anywhere = pl.BlockSpec(memory_space=pl.ANY)
    size = 4 * (features.size + curvature.size)
    return pl.pallas_call(
        load_kernel,
        in_specs=[anywhere, anywhere],
        out_specs=[anywhere, anywhere],
        out_shape=[
            jax.ShapeDtypeStruct(features.shape, features.dtype),
            jax.ShapeDtypeStruct(curvature.shape, curvature.dtype),
        ],
        scratch_shapes=[pltpu.SemaphoreType.DMA((2,))],
        compiler_params=pltpu.CompilerParams(vmem_limit_bytes=2**20),
        cost_estimate=pl.CostEstimate(flops=0, bytes_accessed=size, transcendentals=0),
    )(features, curvature)


def curve(features, curvature, chunk, blocks, halves, n_dp):
    tokens, din = features.shape
    width = halves[0].shape[1]
    tile = TILE if tokens % TILE == 0 else tokens
    flops = 4 * tokens * din * width
    size = 2 * tokens * (din + width) + 6 * din * width
    half = pl.BlockSpec((din // 2, width), lambda i, blocks: (0, 0))
    return pl.pallas_call(
        lambda *refs: curve_kernel(*refs, n_dp=n_dp, token_count=n_dp * tokens),
        grid_spec=pltpu.PrefetchScalarGridSpec(
            num_scalar_prefetch=1,
            grid=(tokens // tile,),
            in_specs=[
                pl.BlockSpec((tile, din), lambda i, blocks: (i, 0)),
                pl.BlockSpec((tile, width), lambda i, blocks: (i, chunk)),
                half,
                half,
            ],
            out_specs=[
                pl.BlockSpec((din, width), lambda i, blocks: (0, 0)),
                pl.BlockSpec((8, width), lambda i, blocks: (0, 0)),
            ],
            scratch_shapes=[
                pltpu.VMEM((din, width), jnp.bfloat16),
                pltpu.VMEM((din, width), jnp.float32),
            ],
        ),
        out_shape=[
            jax.ShapeDtypeStruct((din, width), jnp.float32),
            jax.ShapeDtypeStruct((8, width), jnp.float32),
        ],
        compiler_params=pltpu.CompilerParams(vmem_limit_bytes=VMEM_LIMIT),
        cost_estimate=pl.CostEstimate(flops=flops, bytes_accessed=size, transcendentals=0),
    )(blocks, features, curvature, *halves)


def shards(features, curvature, task_grad):
    n_dp = lax.axis_size("dp")
    din = features.shape[1]
    token_count = features.shape[0] * n_dp
    width = task_grad.shape[1] // CHUNKS
    me = lax.axis_index("dp")
    odd = lax.axis_index("mp") % 2
    blocks = jnp.where(odd, *[jnp.array(order_of(r), jnp.int32) for r in routes()[::-1]]) ^ me
    steps = len(strides_of("dp"))
    chunks = range(CHUNKS)
    hops = []
    dots = None

    def multiply(k, halves):
        rows, stats = curve(features, curvature, k, blocks, halves, n_dp)
        return rows, stats

    tie = lax.optimization_barrier

    def in_step(moving):
        arrived = tie([m[-1] for m in moving])
        return [(*m[:-1], a) for m, a in zip(moving, arrived)]

    def hop():
        nonlocal dots
        if hops:
            dots = dots + swap(dots, *hops.pop(0))

    features, curvature = load(features, curvature)
    grad = [task_grad[:, k * width : (k + 1) * width] for k in chunks]

    held = list(tie([g.astype(jnp.bfloat16) for g in grad]))
    for step in range(steps):
        grad_rows = [(h, trade(h, step)) for h in held]
        if step + 1 < steps:
            held = [join(pair) for pair in grad_rows]

    stats, moving = [None] * CHUNKS, [None] * CHUNKS
    for k in chunks:
        rows, stats[k] = multiply(k, grad_rows[k])
        moving[k] = scatter_start(rows, stats[k][3:4], steps - 1)
    image, guess, lift = [None] * CHUNKS, [None] * CHUNKS, [None] * CHUNKS
    bound = bound_of(din)
    for step in reversed(range(steps)):
        for k in chunks:
            total, extra = scatter_end(*moving[k])
            if step:
                moving[k] = scatter_start(total, extra, step - 1)
                moving[k : k + 2] = in_step(moving[k : k + 2])
                continue
            image[k] = total / (stats[k][2:3] * token_count) + damp_coef * grad[k]
            guess[k] = 1.0 / (extra * (bound / WIRE_MAX) + damp_coef)
            reach = jnp.maximum(stats[k][1:2], TINY) * (1.0 + 2.0 * (bound + 1.0))
            lift[k] = WIRE_MAX / reach
            trial = ((grad[k] - guess[k] * image[k]) * lift[k]).astype(WIRE)
            moving[k] = (trial, trade(trial, 0))
            moving[k : k + 2] = in_step(moving[k : k + 2])

    dots = jnp.concatenate(
        [
            sum(colsum(grad[k] * grad[k]) for k in chunks),
            sum(colsum(grad[k] * image[k]) for k in chunks),
            sum(colsum(image[k] * image[k]) for k in chunks),
        ]
    )
    all_hops = [(axis, stride) for axis in ("mp", "dp") for stride in reversed(strides_of(axis))]
    hops = list(all_hops)
    for step in range(1, steps):
        for k in chunks:
            held = join(moving[k])
            moving[k] = (held, trade(held, step))
            moving[k : k + 2] = in_step(moving[k : k + 2])
    while hops:
        hop()
    coef = pl.pallas_call(
        coef_kernel, out_shape=jax.ShapeDtypeStruct((8 * CHUNKS, width), jnp.float32)
    )(dots, *[row for k in chunks for row in (guess[k], lift[k])])

    direction = []
    for k in chunks:
        row = coef[8 * k : 8 * k + 8]
        direction.append(row[3:4] * grad[k] - row[2:3] * image[k])
        halves = [
            (row[0:1] * t.astype(jnp.float32) + row[1:2] * g.astype(jnp.float32)).astype(
                jnp.bfloat16
            )
            for t, g in zip(moving[k], grad_rows[k])
        ]
        rows, stats[k] = multiply(k, halves)
        moving[k] = scatter_start(rows, None, steps - 1)

    dots = sum(s[0:1] for s in stats) / token_count
    dots += damp_coef * sum(colsum(d * d) for d in direction)
    hops = list(all_hops)
    hop()
    for step in reversed(range(steps)):
        for k in chunks:
            kept, _, received = moving[k]
            if hops:
                received, dots = tie((received, dots))
                hop()
            total, _ = scatter_end(kept, None, received)
            if step:
                moving[k] = scatter_start(total, None, step - 1)
            else:
                moving[k] = total / (stats[k][2:3] * token_count)
    while hops:
        hop()
    direction_dot = jnp.sum(dots, axis=1, keepdims=True)
    solution, residual = [], []
    for k in chunks:
        row = coef[8 * k : 8 * k + 8]
        last_len = row[4:5] / direction_dot
        curved = moving[k] + damp_coef * direction[k]
        solution.append(row[2:3] * grad[k] + last_len * direction[k])
        residual.append(grad[k] - row[2:3] * image[k] - last_len * curved)
    return jnp.concatenate(solution, axis=1), jnp.concatenate(residual, axis=1)


def solution(mesh):
    placed = (P("dp", None), P("dp", "mp"), P("dp", "mp"))
    return jax.shard_map(
        shards,
        mesh=mesh,
        in_specs=placed,
        out_specs=(P("dp", "mp"), P("dp", "mp")),
        check_vma=False,
    )
```

```python
import jax
import jax.numpy as jnp
from jax import lax
from jax.experimental import pallas as pl
from jax.experimental.pallas import tpu as pltpu
from jax.sharding import PartitionSpec as P

CHUNKS = 2
TILE = 1536
VMEM_LIMIT = 28 * 2**20

damp_coef = 0.5

FEATURE_MAX = 6.0
CURVATURE_MAX = 2.0
WIRE = jnp.float16
WIRE_MAX = 32768.0
TINY = 1e-30
EXTRA = 16


def swap(values, axis, stride):
    size = lax.axis_size(axis)
    return lax.ppermute(values, axis, [(i, i ^ stride) for i in range(size)])


def strides_of(axis):
    size = lax.axis_size(axis)
    return [1 << bit for bit in reversed(range(size.bit_length() - 1))]


def routes():
    even = strides_of("dp")
    odd = even[:-2] + even[:-3:-1]
    return even, odd


def trade(values, step):
    n_dp, n_mp = lax.axis_size("dp"), lax.axis_size("mp")
    pairs = []
    for d in range(n_dp):
        for m in range(n_mp):
            pairs.append((d * n_mp + m, (d ^ routes()[m % 2][step]) * n_mp + m))
    return lax.ppermute(values, ("dp", "mp"), pairs)


def order_of(route):
    order = [0]
    for stride in route:
        order = order + [place ^ stride for place in order]
    return order


def join(halves):
    return jnp.concatenate(halves, axis=0)


def scatter_start(total, extra, step):
    half = total.shape[0] // 2
    sent = total[half:].astype(WIRE)
    if extra is not None:
        extra = extra.astype(WIRE)
        sent = join([sent, jnp.broadcast_to(extra, (EXTRA, extra.shape[1]))])
    return total[:half], extra, trade(sent, step)


def scatter_end(kept, extra, received):
    half = kept.shape[0]
    total = kept + received[:half].astype(jnp.float32)
    if extra is not None:
        extra = extra.astype(jnp.float32) + received[half : half + 1].astype(jnp.float32)
    return total, extra


def colsum(values):
    return jnp.sum(values, axis=0, keepdims=True)


def coef_kernel(sums_ref, *refs):
    out_ref = refs[-1]
    total = jnp.sum(sums_ref[...], axis=1, keepdims=True)
    norm, curv, image = total[0:1], total[1:2], total[2:3]
    step = norm / curv
    following = norm - 2.0 * step * curv + step * step * image
    ratio = following / norm
    width = sums_ref.shape[1]
    for k, (guess_ref, lift_ref) in enumerate(zip(refs[:-1:2], refs[1:-1:2])):
        along = step / guess_ref[...]
        out_ref[8 * k : 8 * k + 1, :] = along / lift_ref[...]
        out_ref[8 * k + 1 : 8 * k + 2, :] = 1.0 + ratio - along
        out_ref[8 * k + 2 : 8 * k + 3, :] = jnp.broadcast_to(step, (1, width))
        out_ref[8 * k + 3 : 8 * k + 4, :] = jnp.broadcast_to(1.0 + ratio, (1, width))
        out_ref[8 * k + 4 : 8 * k + 5, :] = jnp.broadcast_to(following, (1, width))


def curve_kernel(blocks, f_ref, c_ref, near_ref, far_ref, out_ref, stat_ref, held, total, *, n_dp, token_count):
    din = total.shape[0]
    rows = din // n_dp
    step = pl.program_id(0)
    last = pl.num_programs(0) - 1

    def place(position):
        return pl.ds(pl.multiple_of(blocks[position] * rows, rows), rows)

    @pl.when(step == 0)
    def _():
        for position in range(n_dp):
            half = (near_ref, far_ref)[2 * position // n_dp]
            at = (position % (n_dp // 2)) * rows
            held[place(position), :] = half[at : at + rows, :]

    projected = jnp.dot(f_ref[...], held[...], preferred_element_type=jnp.float32)
    weighted = (c_ref[...].astype(jnp.float32) * projected).astype(jnp.bfloat16)
    share = lax.dot_general(
        f_ref[...], weighted, (((0,), (0,)), ((), ())), preferred_element_type=jnp.float32
    )

    @pl.when(step == 0)
    def _():
        total[...] = share

    @pl.when(step > 0)
    def _():
        total[...] += share

    @pl.when(step == last)
    def _():
        vector = held[...].astype(jnp.float32)
        dot = jnp.sum(vector * total[...], axis=0, keepdims=True)
        largest = jnp.max(jnp.abs(vector), axis=0, keepdims=True)
        to_wire = WIRE_MAX / (bound_of(din) * token_count)
        square = jnp.sum(vector * vector, axis=0, keepdims=True)
        scale = to_wire / jnp.maximum(largest, TINY)
        stat_ref[0:1, :] = dot
        stat_ref[1:2, :] = largest
        stat_ref[2:3, :] = scale
        stat_ref[3:4, :] = dot / jnp.maximum(square, TINY) * to_wire
        for position in range(n_dp):
            out_ref[position * rows : (position + 1) * rows, :] = total[place(position), :] * scale


def bound_of(din):
    return FEATURE_MAX * FEATURE_MAX * CURVATURE_MAX * din


def load_kernel(f_ref, c_ref, f_out, c_out, sems):
    copies = [
        pltpu.make_async_copy(f_ref, f_out, sems.at[0]),
        pltpu.make_async_copy(c_ref, c_out, sems.at[1]),
    ]
    for copy in copies:
        copy.start()
    for copy in copies:
        copy.wait()


def load(features, curvature):
    anywhere = pl.BlockSpec(memory_space=pl.ANY)
    size = 4 * (features.size + curvature.size)
    return pl.pallas_call(
        load_kernel,
        in_specs=[anywhere, anywhere],
        out_specs=[anywhere, anywhere],
        out_shape=[
            jax.ShapeDtypeStruct(features.shape, features.dtype),
            jax.ShapeDtypeStruct(curvature.shape, curvature.dtype),
        ],
        scratch_shapes=[pltpu.SemaphoreType.DMA((2,))],
        compiler_params=pltpu.CompilerParams(vmem_limit_bytes=2**20),
        cost_estimate=pl.CostEstimate(flops=0, bytes_accessed=size, transcendentals=0),
    )(features, curvature)


def curve(features, curvature, chunk, blocks, halves, n_dp):
    tokens, din = features.shape
    width = halves[0].shape[1]
    tile = TILE if tokens % TILE == 0 else tokens
    flops = 4 * tokens * din * width
    size = 2 * tokens * (din + width) + 6 * din * width
    half = pl.BlockSpec((din // 2, width), lambda i, blocks: (0, 0))
    return pl.pallas_call(
        lambda *refs: curve_kernel(*refs, n_dp=n_dp, token_count=n_dp * tokens),
        grid_spec=pltpu.PrefetchScalarGridSpec(
            num_scalar_prefetch=1,
            grid=(tokens // tile,),
            in_specs=[
                pl.BlockSpec((tile, din), lambda i, blocks: (i, 0)),
                pl.BlockSpec((tile, width), lambda i, blocks: (i, chunk)),
                half,
                half,
            ],
            out_specs=[
                pl.BlockSpec((din, width), lambda i, blocks: (0, 0)),
                pl.BlockSpec((8, width), lambda i, blocks: (0, 0)),
            ],
            scratch_shapes=[
                pltpu.VMEM((din, width), jnp.bfloat16),
                pltpu.VMEM((din, width), jnp.float32),
            ],
        ),
        out_shape=[
            jax.ShapeDtypeStruct((din, width), jnp.float32),
            jax.ShapeDtypeStruct((8, width), jnp.float32),
        ],
        compiler_params=pltpu.CompilerParams(vmem_limit_bytes=VMEM_LIMIT),
        cost_estimate=pl.CostEstimate(flops=flops, bytes_accessed=size, transcendentals=0),
    )(blocks, features, curvature, *halves)


def shards(features, curvature, task_grad):
    n_dp = lax.axis_size("dp")
    din = features.shape[1]
    token_count = features.shape[0] * n_dp
    width = task_grad.shape[1] // CHUNKS
    me = lax.axis_index("dp")
    odd = lax.axis_index("mp") % 2
    blocks = jnp.where(odd, *[jnp.array(order_of(r), jnp.int32) for r in routes()[::-1]]) ^ me
    steps = len(strides_of("dp"))
    chunks = range(CHUNKS)
    hops = []
    dots = None

    def multiply(k, halves):
        rows, stats = curve(features, curvature, k, blocks, halves, n_dp)
        return rows, stats

    tie = lax.optimization_barrier

    def in_step(moving):
        arrived = tie([m[-1] for m in moving])
        return [(*m[:-1], a) for m, a in zip(moving, arrived)]

    def hop():
        nonlocal dots
        if hops:
            dots = dots + swap(dots, *hops.pop(0))

    features, curvature = load(features, curvature)
    grad = [task_grad[:, k * width : (k + 1) * width] for k in chunks]

    held = [g.astype(jnp.bfloat16) for g in grad]
    for step in range(steps):
        grad_rows = [(h, trade(h, step)) for h in held]
        if step + 1 < steps:
            held = [join(pair) for pair in grad_rows]

    stats, moving = [None] * CHUNKS, [None] * CHUNKS
    for k in chunks:
        rows, stats[k] = multiply(k, grad_rows[k])
        moving[k] = scatter_start(rows, stats[k][3:4], steps - 1)
    image, guess, lift = [None] * CHUNKS, [None] * CHUNKS, [None] * CHUNKS
    bound = bound_of(din)
    for step in reversed(range(steps)):
        for k in chunks:
            total, extra = scatter_end(*moving[k])
            if step:
                moving[k] = scatter_start(total, extra, step - 1)
                moving[k : k + 2] = in_step(moving[k : k + 2])
                continue
            image[k] = total / (stats[k][2:3] * token_count) + damp_coef * grad[k]
            guess[k] = 1.0 / (extra * (bound / WIRE_MAX) + damp_coef)
            reach = jnp.maximum(stats[k][1:2], TINY) * (1.0 + 2.0 * (bound + 1.0))
            lift[k] = WIRE_MAX / reach
            trial = ((grad[k] - guess[k] * image[k]) * lift[k]).astype(WIRE)
            moving[k] = (trial, trade(trial, 0))
            moving[k : k + 2] = in_step(moving[k : k + 2])

    dots = jnp.concatenate(
        [
            sum(colsum(grad[k] * grad[k]) for k in chunks),
            sum(colsum(grad[k] * image[k]) for k in chunks),
            sum(colsum(image[k] * image[k]) for k in chunks),
        ]
    )
    all_hops = [(axis, stride) for axis in ("mp", "dp") for stride in reversed(strides_of(axis))]
    hops = list(all_hops)
    for step in range(1, steps):
        for k in chunks:
            held = join(moving[k])
            moving[k] = (held, trade(held, step))
            if step + 1 < steps:
                moving[k : k + 2] = in_step(moving[k : k + 2])
    while hops:
        hop()
    coef = pl.pallas_call(
        coef_kernel, out_shape=jax.ShapeDtypeStruct((8 * CHUNKS, width), jnp.float32)
    )(dots, *[row for k in chunks for row in (guess[k], lift[k])])

    direction = []
    for k in chunks:
        row = coef[8 * k : 8 * k + 8]
        direction.append(row[3:4] * grad[k] - row[2:3] * image[k])
        halves = [
            (row[0:1] * t.astype(jnp.float32) + row[1:2] * g.astype(jnp.float32)).astype(
                jnp.bfloat16
            )
            for t, g in zip(moving[k], grad_rows[k])
        ]
        rows, stats[k] = multiply(k, halves)
        moving[k] = scatter_start(rows, None, steps - 1)

    dots = sum(s[0:1] for s in stats) / token_count
    dots += damp_coef * sum(colsum(d * d) for d in direction)
    hops = list(all_hops)
    hop()
    for step in reversed(range(steps)):
        for k in chunks:
            kept, _, received = moving[k]
            if hops:
                received, dots = tie((received, dots))
                hop()
            total, _ = scatter_end(kept, None, received)
            if step:
                moving[k] = scatter_start(total, None, step - 1)
            else:
                moving[k] = total / (stats[k][2:3] * token_count)
    while hops:
        hop()
    direction_dot = jnp.sum(dots, axis=1, keepdims=True)
    solution, residual = [], []
    for k in chunks:
        row = coef[8 * k : 8 * k + 8]
        last_len = row[4:5] / direction_dot
        curved = moving[k] + damp_coef * direction[k]
        solution.append(row[2:3] * grad[k] + last_len * direction[k])
        residual.append(grad[k] - row[2:3] * image[k] - last_len * curved)
    return jnp.concatenate(solution, axis=1), jnp.concatenate(residual, axis=1)


def solution(mesh):
    placed = (P("dp", None), P("dp", "mp"), P("dp", "mp"))
    return jax.shard_map(
        shards,
        mesh=mesh,
        in_specs=placed,
        out_specs=(P("dp", "mp"), P("dp", "mp")),
        check_vma=False,
    )
```
